32 devices in a mesh: seq: 16 (over z, y, core), head: 2 (over x).
Axes of the slice: x: 2, y: 2, z: 4, core: 2. Of those that a mesh axis runs over, the one named last changes fastest.
Arguments:
- queries: bfloat16 [16384, 1024], P('seq', 'head'), may hold values from -6 to 6
- keys: bfloat16 [16384, 1024], P('seq', 'head'), may hold values from -6 to 6
- values: bfloat16 [16384, 1024], P('seq', 'head'), may hold values from -6 to 6
- gates: bfloat16 [16384, 1024], P('seq', 'head'), may hold values from -6 to 6
- sessions: int32 [16384], P('seq'), may hold values from 0 to 7, never falling along the last dimension, each value on 1 to 3072 neighbouring positions
- score_bias: float32 [8], P('head'), may hold values from -1 to 1
- grad_out: bfloat16 [16384, 1024], P('seq', 'head'), may hold values from -6 to 6
- w_out: bfloat16 [1024, 1024], P('head'), may hold values from -0.1875 to 0.1875
Outputs:
- grad_queries: float32 [16384, 1024], P('seq', 'head')
- grad_keys: float32 [16384, 1024], P('seq', 'head')
- grad_values: float32 [16384, 1024], P('seq', 'head')
- grad_gates: float32 [16384, 1024], P('seq', 'head')
- grad_w_out: float32 [1024, 1024], P('head', 'seq')
The draws below stay inside these ranges and needn't reach their ends.
Inputs may be any that keep to these rules, and one draw needn't show every extreme that they name: `sessions`: session numbers never fall from one event to the next; every session number is used, each session has 1 to 3072 events and one has exactly 3072.
All inputs are finite; a program needn't handle non-finite values.
Results may differ from the reference program's by a relative error of at most 0.0042.
Values may be sent and summed in bfloat16 or wider, within the bound.
A program may use at most 192 MiB of HBM per device.

```python
import math
import jax
import jax.numpy as jnp
import numpy as np
from jax import lax

H = 8
DH = 128
D = 1024
TOK_DEV = 1024
TOKENS = 16384
SESS_MAX = 3072
SESSIONS = 8


def raised(entries, rng, source, target, shards_of, factor):
    def block_of(position):
        return (jnp.arange(entries.shape[position]) // (entries.shape[position] // shards_of)).reshape((-1,) + (1,) * (entries.ndim - 1 - position))

    one_side = jax.random.permutation(rng, shards_of)[block_of(target)]
    second = (block_of(target) + shards_of // 2) % shards_of
    return jnp.where((block_of(source) == one_side) | (block_of(source) == second), factor * entries, entries)


def block_levels(rng, shape, pieces, least, largest):
    gain, own = 1.0, jax.random.fold_in(rng, 6)
    for position, blocks in pieces:
        draws = jnp.exp(jax.random.uniform(jax.random.fold_in(own, position), (blocks,), jnp.float32, least / len(pieces), largest / len(pieces)))
        gain = gain * jnp.repeat(draws, shape[position] // blocks).reshape([-1 if axis == position else 1 for axis in range(len(shape))])
    return gain


def split_up(count, total, bound, lean):
    portions = [(1 << 20) // math.isqrt(rank ** lean) + 1 for rank in range(2, count + 1)]
    surplus, holding = total - bound - (count - 1), [1] * (count - 1)
    while surplus > 0:
        candidates = [i for i in range(count - 1) if holding[i] < bound]
        mass, budget = sum([portions[i] for i in candidates]), surplus
        for i in candidates:
            more = min(bound - holding[i], max(1, budget * portions[i] // mass), surplus)
            holding[i] = holding[i] + more
            surplus = surplus - more
    return np.array([bound] + holding)


def uneven_parts(rng, amount, total, most, lean):
    if amount == 2:
        one = jax.random.randint(rng, (), max(1, total - most), min(most, total - 1) + 1)
        return jnp.stack([one, total - one])
    sizes = jnp.asarray(split_up(amount, total, most, lean), jnp.int32)
    twos = (amount - 1) // 2
    giver, taker = sizes[1:1 + 2 * twos:2], sizes[2:2 + 2 * twos:2]
    slack = jnp.minimum(giver - 1, most - taker)
    shifted = jax.random.randint(jax.random.fold_in(rng, 1), (twos,), 0, 1 << 20) % (slack + 1)
    sizes = sizes.at[1:1 + 2 * twos:2].set(giver - shifted).at[2:2 + 2 * twos:2].set(taker + shifted)
    return sizes[jax.random.permutation(jax.random.fold_in(rng, 2), amount)]


def noise(own_key, dims, width, bound, cuts=(), held_as=jnp.bfloat16):
    loudness = block_levels(own_key, dims, cuts, -0.22, 0.18) if cuts else 1.0
    array = jax.random.normal(own_key, dims, jnp.float32) * width * loudness
    return jnp.minimum(jnp.maximum(array, -bound), bound).astype(held_as)


def noise_with(stream_key, extent, deviation, bound, split, heavy, kind=jnp.bfloat16):
    entries = deviation * jax.random.normal(stream_key, extent, jnp.float32)
    if split:
        entries = entries * block_levels(stream_key, extent, split, -0.22, 0.18)
    return jnp.clip(raised(entries, jax.random.fold_in(stream_key, 3), *heavy), -bound, bound).astype(kind)


def setup_inputs(seed: int = 0) -> dict:
    key_of = jax.random.split(jax.random.key(seed), 9)
    return {
        "queries": noise(key_of[0], (TOKENS, D), 1.0, 6.0, ((0, 16), (1, 2))),
        "keys": noise(key_of[1], (TOKENS, D), 1.0, 6.0, ((0, 16), (1, 2))),
        "values": noise(key_of[2], (TOKENS, D), 1.0, 6.0, ((0, 16), (1, 2))),
        "gates": noise(key_of[3], (TOKENS, D), 1.0, 6.0, ((0, 16), (1, 2))),
        "sessions": jnp.searchsorted(jnp.cumsum(uneven_parts(key_of[4], SESSIONS, TOKENS, SESS_MAX, 2)), jnp.arange(TOKENS), side="right").astype(jnp.int32),
        "score_bias": jnp.clip(jax.random.uniform(key_of[5], (H,), jnp.float32, -1.0, 1.0) * block_levels(key_of[5], (H,), ((0, 2),), -0.4, 0.0), -1.0, 1.0),
        "grad_out": noise_with(key_of[6], (TOKENS, D), 1.0, 6.0, ((0, 16), (1, 2)), (0, 1, 16, 2.0)),
        "w_out": noise(key_of[7], (D, D), D ** -0.5, 0.1875, ((0, 2),)),
    }


def silu_parts(scores):
    sigma = jax.nn.sigmoid(scores)
    return (scores * sigma, sigma * (1.0 + scores * (1.0 - sigma)))

def reference(queries, keys, values, gates, sessions, score_bias, grad_out, w_out):
    event_count = queries.shape[0]
    back_rows = 3 * TOK_DEV
    scale = 1.0 / math.sqrt(DH)
    block_count = event_count // TOK_DEV
    q_heads = queries.astype(jnp.float32).reshape(event_count, H, DH)
    k_heads = keys.astype(jnp.float32).reshape(event_count, H, DH)
    v_heads = values.astype(jnp.float32).reshape(event_count, H, DH)
    pad_rows = jnp.zeros((back_rows, H, DH), jnp.float32)
    keys_padded = jnp.concatenate([pad_rows, k_heads], 0)
    values_padded = jnp.concatenate([pad_rows, v_heads], 0)
    sessions_padded = jnp.concatenate([jnp.full((back_rows,), -1, jnp.int32), sessions.astype(jnp.int32)], 0)
    bias_col = score_bias.astype(jnp.float32).reshape(H, 1, 1)
    local_pos = jnp.arange(TOK_DEV, dtype=jnp.int32)
    window_pos = jnp.arange(4 * TOK_DEV, dtype=jnp.int32) - back_rows

    def block_setup(block_index):
        first_row = (block_index * TOK_DEV).astype(jnp.int32)
        q_block = lax.dynamic_slice_in_dim(q_heads, first_row, TOK_DEV, 0)
        k_block = lax.dynamic_slice_in_dim(keys_padded, first_row, 4 * TOK_DEV, 0)
        v_block = lax.dynamic_slice_in_dim(values_padded, first_row, 4 * TOK_DEV, 0)
        key_sessions = lax.dynamic_slice_in_dim(sessions_padded, first_row, 4 * TOK_DEV, 0)
        query_sessions = lax.dynamic_slice_in_dim(sessions.astype(jnp.int32), first_row, TOK_DEV, 0)
        allowed = (query_sessions[:, None] == key_sessions[None, :]) & (window_pos[None, :] <= local_pos[:, None])
        scores = jnp.einsum('ihd,jhd->hij', q_block, k_block, precision=lax.Precision.HIGHEST) * scale + bias_col
        return (first_row, q_block, k_block, v_block, allowed, scores)

    def forward_block(block_index):
        first_row, q_block, k_block, v_block, allowed, scores = block_setup(block_index)
        act, deriv = silu_parts(scores)
        weights = jnp.where(allowed[None], act, 0.0).astype(jnp.bfloat16).astype(jnp.float32)
        return jnp.einsum('hij,jhd->ihd', weights, v_block, precision=lax.Precision.HIGHEST)
    block_ids = jnp.arange(block_count, dtype=jnp.int32)
    attended = lax.map(forward_block, block_ids).reshape(event_count, H, DH)
    centered = attended - lax.optimization_barrier(jnp.mean(attended, axis=-1, keepdims=True))
    inv_std = lax.rsqrt(lax.optimization_barrier(jnp.mean(centered * centered, axis=-1, keepdims=True)) + 1e-05)
    normed = centered * inv_std
    gate_heads = gates.astype(jnp.float32).reshape(event_count, H, DH)
    mixed = (normed * gate_heads).astype(jnp.bfloat16).reshape(event_count, H * DH)
    grad_mixed = jnp.dot(grad_out, w_out.T, preferred_element_type=jnp.float32).reshape(event_count, H, DH)
    grad_gates = (grad_mixed * normed).reshape(event_count, H * DH)
    grad_normed = grad_mixed * gate_heads
    grad_attended = (grad_normed - lax.optimization_barrier(jnp.mean(grad_normed, axis=-1, keepdims=True)) - normed * lax.optimization_barrier(jnp.mean(grad_normed * normed, axis=-1, keepdims=True))) * inv_std
    grad_attended = grad_attended.astype(jnp.bfloat16).astype(jnp.float32)

    def backward_block(accum, block_index):
        grad_keys_pad, grad_values_pad = accum
        first_row, q_block, k_block, v_block, allowed, scores = block_setup(block_index)
        act, deriv = silu_parts(scores)
        weights = jnp.where(allowed[None], act, 0.0).astype(jnp.bfloat16).astype(jnp.float32)
        grad_block = lax.dynamic_slice_in_dim(grad_attended, first_row, TOK_DEV, 0)
        values_term = jnp.einsum('hij,ihd->jhd', weights, grad_block, precision=lax.Precision.HIGHEST)
        grad_weights = jnp.einsum('ihd,jhd->hij', grad_block, v_block, precision=lax.Precision.HIGHEST)
        grad_scores = jnp.where(allowed[None], grad_weights * deriv * scale, 0.0).astype(jnp.bfloat16).astype(jnp.float32)
        query_term = jnp.einsum('hij,jhd->ihd', grad_scores, k_block, precision=lax.Precision.HIGHEST)
        keys_term = jnp.einsum('hij,ihd->jhd', grad_scores, q_block, precision=lax.Precision.HIGHEST)
        old_keys = lax.dynamic_slice_in_dim(grad_keys_pad, first_row, 4 * TOK_DEV, 0)
        old_values = lax.dynamic_slice_in_dim(grad_values_pad, first_row, 4 * TOK_DEV, 0)
        grad_keys_pad = lax.dynamic_update_slice_in_dim(grad_keys_pad, old_keys + keys_term, first_row, 0)
        grad_values_pad = lax.dynamic_update_slice_in_dim(grad_values_pad, old_values + values_term, first_row, 0)
        return ((grad_keys_pad, grad_values_pad), query_term)
    start_accum = (jnp.zeros((event_count + back_rows, H, DH), jnp.float32), jnp.zeros((event_count + back_rows, H, DH), jnp.float32))
    (grad_keys_pad, grad_values_pad), query_terms = lax.scan(backward_block, start_accum, block_ids)
    grad_queries = query_terms.reshape(event_count, H * DH)
    grad_keys = grad_keys_pad[back_rows:].reshape(event_count, H * DH)
    grad_values = grad_values_pad[back_rows:].reshape(event_count, H * DH)
    grad_w_out = jnp.dot(mixed.T, grad_out, preferred_element_type=jnp.float32)
    return (grad_queries, grad_keys, grad_values, grad_gates, grad_w_out)
```

```python
import functools
import math

import jax
import jax.numpy as jnp
from jax import lax
from jax.experimental import pallas as pl
from jax.experimental.pallas import tpu as pltpu
from jax.sharding import PartitionSpec as P

DH = 128
BLOCK = 256

back_steps = (1, 2, 3)
norm_eps = 1e-05
half_scale = 0.5 / math.sqrt(DH)


def shifted(block, axis, distance):
    devices = range(lax.axis_size(axis))
    route = [(i - distance, i) for i in devices if i - distance in devices]
    return lax.ppermute(block, axis, route)


def nt(a, b):
    return lax.dot_general(a, b, (((1,), (1,)), ((), ())), preferred_element_type=jnp.float32)


def nn(a, b):
    return lax.dot_general(a, b, (((1,), (0,)), ((), ())), preferred_element_type=jnp.float32)


def tn(a, b):
    return lax.dot_general(a, b, (((0,), (0,)), ((), ())), preferred_element_type=jnp.float32)


def rows_of(index):
    return pl.ds(pl.multiple_of(index * BLOCK, BLOCK), BLOCK)


def head_cols(h):
    return slice(h * DH, (h + 1) * DH)


def each_pair(own, n_q, n_k, lo_ref, body):
    def over_q(qi, carry):
        def over_k(kj, inner):
            body(qi, kj)
            return inner

        lax.fori_loop(lo_ref[qi], qi + 1 if own else n_k, over_k, 0)
        return carry

    lax.fori_loop(0, n_q, over_q, 0)


def forward_kernel(own, heads, lo_ref, bias_ref, q_ref, k_ref, v_ref, sq_ref, sk_ref, *rest):
    out_ref = rest[-1]
    if own:
        out_ref[...] = jnp.zeros_like(out_ref)
    else:
        out_ref[...] = rest[0][...]

    def body(qi, kj):
        rq, rk = rows_of(qi), rows_of(kj)
        allowed = sq_ref[rq, :] == sk_ref[kj]
        if own:
            i = lax.broadcasted_iota(jnp.int32, (BLOCK, BLOCK), 0) + qi * BLOCK
            j = lax.broadcasted_iota(jnp.int32, (BLOCK, BLOCK), 1) + kj * BLOCK
            allowed = allowed & (j <= i)
        for h in range(heads):
            c = head_cols(h)
            half = nt(q_ref[rq, c], k_ref[rk, c]) * half_scale + 0.5 * bias_ref[h]
            act = half * jnp.tanh(half) + half
            weights = jnp.where(allowed, act, 0.0).astype(jnp.bfloat16)
            out_ref[rq, c] += nn(weights, v_ref[rk, c])

    each_pair(own, q_ref.shape[0] // BLOCK, k_ref.shape[0] // BLOCK, lo_ref, body)


def backward_kernel(
    own, heads, lo_ref, bias_ref, q_ref, k_ref, v_ref, ga_ref, sq_ref, sk_ref, *rest
):
    if own:
        dq_in, dq_ref, dk_ref, dv_ref = rest
        dk_acc, dv_acc = dk_ref, dv_ref
        dq_ref[...] = dq_in[...]
    elif len(rest) == 5:
        dq_ref, dk_ref, dv_ref, dk_acc, dv_acc = rest
        dq_ref[...] = jnp.zeros_like(dq_ref)
    else:
        dq_in, dq_ref, dk_ref, dv_ref, dk_acc, dv_acc = rest
        dq_ref[...] = dq_in[...]
    dk_acc[...] = jnp.zeros_like(dk_acc)
    dv_acc[...] = jnp.zeros_like(dv_acc)

    def body(qi, kj):
        rq, rk = rows_of(qi), rows_of(kj)
        allowed = sk_ref[rk, :] == sq_ref[qi]
        if own:
            j = lax.broadcasted_iota(jnp.int32, (BLOCK, BLOCK), 0) + kj * BLOCK
            i = lax.broadcasted_iota(jnp.int32, (BLOCK, BLOCK), 1) + qi * BLOCK
            allowed = allowed & (j <= i)
        for h in range(heads):
            c = head_cols(h)
            q, k, ga = q_ref[rq, c], k_ref[rk, c], ga_ref[rq, c]
            half = nt(k, q) * half_scale + 0.5 * bias_ref[h]
            up = jnp.tanh(half) + 1.0
            act = half * up
            weights = jnp.where(allowed, act, 0.0).astype(jnp.bfloat16)
            dv_acc[rk, c] += nn(weights, ga)
            slope = (act * (2.0 - up) + up) * half_scale
            grad_scores = jnp.where(allowed, nt(v_ref[rk, c], ga) * slope, 0.0).astype(jnp.bfloat16)
            dk_acc[rk, c] += nn(grad_scores, q)
            dq_ref[rq, c] += tn(grad_scores, k)

    each_pair(own, q_ref.shape[0] // BLOCK, k_ref.shape[0] // BLOCK, lo_ref, body)
    if not own:
        dk_ref[...] = dk_acc[...].astype(dk_ref.dtype)
        dv_ref[...] = dv_acc[...].astype(dv_ref.dtype)


vmem = pl.BlockSpec(memory_space=pltpu.VMEM)
smem = pl.BlockSpec(memory_space=pltpu.SMEM)
kernel_params = pltpu.CompilerParams(vmem_limit_bytes=50 * 1024 * 1024)


def window_cost(own, rows, features, products):
    pairs = rows * rows // (2 if own else 1)
    return pl.CostEstimate(
        flops=4 * products * pairs * features,
        bytes_accessed=10 * rows * features,
        transcendentals=pairs * features // DH,
    )


def forward_window(own, lo, bias, q, k, v, sq_col, sk_row, attended):
    rows, features = q.shape
    extra = () if own else (attended,)
    return pl.pallas_call(
        functools.partial(forward_kernel, own, features // DH),
        out_shape=jax.ShapeDtypeStruct((rows, features), jnp.float32),
        in_specs=[smem, smem] + [vmem] * (5 + len(extra)),
        out_specs=vmem,
        input_output_aliases={} if own else {7: 0},
        compiler_params=kernel_params,
        cost_estimate=window_cost(own, rows, features, 2),
    )(lo, bias, q, k, v, sq_col, sk_row, *extra)


def backward_window(own, lo, bias, q, k, v, ga, sq_row, sk_col, dq):
    rows, features = q.shape
    extra = () if dq is None else (dq,)
    term = jax.ShapeDtypeStruct((rows, features), jnp.float32 if own else jnp.bfloat16)
    scratch = [] if own else [pltpu.VMEM((rows, features), jnp.float32)] * 2
    return pl.pallas_call(
        functools.partial(backward_kernel, own, features // DH),
        out_shape=(jax.ShapeDtypeStruct((rows, features), jnp.float32), term, term),
        in_specs=[smem, smem] + [vmem] * (6 + len(extra)),
        out_specs=(vmem, vmem, vmem),
        scratch_shapes=scratch,
        input_output_aliases={8: 0} if extra else {},
        compiler_params=kernel_params,
        cost_estimate=window_cost(own, rows, features, 5),
    )(lo, bias, q, k, v, ga, sq_row, sk_col, *extra)


def per_device(queries, keys, values, gates, sessions, score_bias, grad_out, w_out):
    rows, features = queries.shape
    heads = features // DH
    blocks = rows // BLOCK
    my_index = lax.axis_index("seq")
    windows = [(keys, values, sessions)]
    for distance in back_steps:
        k, v, s = shifted((keys, values, sessions), "seq", distance)
        windows.append((k, v, jnp.where(my_index >= distance, s, -1)))
    first_of = sessions.reshape(blocks, BLOCK)[:, 0]
    lows = []
    for k, v, s in windows:
        last_of = s.reshape(blocks, BLOCK)[:, -1]
        lows.append(jnp.sum((last_of[None, :] < first_of[:, None]).astype(jnp.int32), axis=1))
    sq_col = sessions.reshape(rows, 1)
    sq_row = sessions.reshape(blocks, 1, BLOCK)

    column_block = lax.all_gather(grad_out, "head", axis=1, tiled=True)
    grad_mixed = nt(column_block, w_out).reshape(rows, heads, DH)

    attended = None
    for distance in (0,) + back_steps:
        k, v, s = windows[distance]
        attended = forward_window(
            distance == 0, lows[distance], score_bias, queries, k, v, sq_col,
            s.reshape(blocks, 1, BLOCK), attended,
        )
    attended = attended.reshape(rows, heads, DH)
    centered = attended - jnp.mean(attended, axis=-1, keepdims=True)
    inv_std = lax.rsqrt(jnp.mean(centered * centered, axis=-1, keepdims=True) + norm_eps)
    normed = centered * inv_std
    gate_heads = gates.reshape(rows, heads, DH).astype(jnp.float32)
    mixed = (normed * gate_heads).astype(jnp.bfloat16).reshape(rows, features)
    grad_gates = (grad_mixed * normed).reshape(rows, features)
    grad_normed = grad_mixed * gate_heads
    grad_attended = (
        grad_normed
        - jnp.mean(grad_normed, axis=-1, keepdims=True)
        - normed * jnp.mean(grad_normed * normed, axis=-1, keepdims=True)
    ) * inv_std
    grad_attended = grad_attended.astype(jnp.bfloat16).reshape(rows, features)
    grad_w_out = lax.psum_scatter(
        tn(mixed, column_block), "seq", scatter_dimension=1, tiled=True
    )

    grad_queries = None
    received = []
    for distance in (3, 2, 1, 0):
        k, v, s = windows[distance]
        grad_queries, dk, dv = backward_window(
            distance == 0, lows[distance], score_bias, queries, k, v, grad_attended, sq_row,
            s.reshape(rows, 1), grad_queries,
        )
        if distance:
            received.append(shifted((dk, dv), "seq", -distance))
    for dk_term, dv_term in received:
        dk = dk + dk_term.astype(jnp.float32)
        dv = dv + dv_term.astype(jnp.float32)
    return grad_queries, dk, dv, grad_gates, grad_w_out


def solution(mesh):
    return jax.shard_map(
        per_device,
        mesh=mesh,
        in_specs=(
            P("seq", "head"),
            P("seq", "head"),
            P("seq", "head"),
            P("seq", "head"),
            P("seq"),
            P("head"),
            P("seq", "head"),
            P("head", None),
        ),
        out_specs=(
            P("seq", "head"),
            P("seq", "head"),
            P("seq", "head"),
            P("seq", "head"),
            P("head", "seq"),
        ),
        check_vma=False,
    )
```

```python
import functools
import math

import jax
import jax.numpy as jnp
from jax import lax
from jax.experimental import pallas as pl
from jax.experimental.pallas import tpu as pltpu
from jax.sharding import PartitionSpec as P

DH = 128
BLOCK = 256

back_steps = (1, 2, 3)
norm_eps = 1e-05
half_scale = 0.5 / math.sqrt(DH)


def shifted(block, axis, distance):
    devices = range(lax.axis_size(axis))
    route = [(i - distance, i) for i in devices if i - distance in devices]
    return lax.ppermute(block, axis, route)


def nt(a, b):
    return lax.dot_general(a, b, (((1,), (1,)), ((), ())), preferred_element_type=jnp.float32)


def nn(a, b):
    return lax.dot_general(a, b, (((1,), (0,)), ((), ())), preferred_element_type=jnp.float32)


def tn(a, b):
    return lax.dot_general(a, b, (((0,), (0,)), ((), ())), preferred_element_type=jnp.float32)


def rows_of(index):
    return pl.ds(pl.multiple_of(index * BLOCK, BLOCK), BLOCK)


def head_cols(h):
    return slice(h * DH, (h + 1) * DH)


def each_pair(own, n_q, n_k, lo_ref, body):
    def over_q(qi, carry):
        def over_k(kj, inner):
            body(qi, kj)
            return inner

        lax.fori_loop(lo_ref[qi], qi + 1 if own else n_k, over_k, 0)
        return carry

    lax.fori_loop(0, n_q, over_q, 0)


def forward_kernel(own, heads, lo_ref, bias_ref, q_ref, kv_ref, sq_ref, sk_ref, *rest):
    rows = q_ref.shape[0]
    out_ref = rest[-1]
    if own:
        out_ref[...] = jnp.zeros_like(out_ref)
    else:
        out_ref[...] = rest[0][...]

    def body(qi, kj):
        rq, rk, rv = rows_of(qi), rows_of(kj), rows_of(kj + rows // BLOCK)
        allowed = sq_ref[rq, :] == sk_ref[kj]
        if own:
            i = lax.broadcasted_iota(jnp.int32, (BLOCK, BLOCK), 0) + qi * BLOCK
            j = lax.broadcasted_iota(jnp.int32, (BLOCK, BLOCK), 1) + kj * BLOCK
            allowed = allowed & (j <= i)
        raws = [nt(q_ref[rq, head_cols(h)], kv_ref[rk, head_cols(h)]) for h in range(heads)]
        for h in range(heads):
            c = head_cols(h)
            half = raws[h] * half_scale + 0.5 * bias_ref[h]
            act = half * jnp.tanh(half) + half
            weights = jnp.where(allowed, act, 0.0).astype(jnp.bfloat16)
            out_ref[rq, c] += nn(weights, kv_ref[rv, c])

    each_pair(own, rows // BLOCK, rows // BLOCK, lo_ref, body)


def backward_kernel(own, heads, lo_ref, bias_ref, q_ref, kv_ref, ga_ref, sq_ref, sk_ref, *rest):
    rows = q_ref.shape[0]
    first = rest[1].dtype == jnp.bfloat16
    if first:
        dq_ref, term_ref, acc = rest
        dq_ref[...] = jnp.zeros_like(dq_ref)
    else:
        dq_in, dq_ref, acc = rest
        dq_ref[...] = dq_in[...]
    acc[...] = jnp.zeros_like(acc)

    def body(qi, kj):
        rq, rk, rv = rows_of(qi), rows_of(kj), rows_of(kj + rows // BLOCK)
        allowed = sk_ref[rk, :] == sq_ref[qi]
        if own:
            j = lax.broadcasted_iota(jnp.int32, (BLOCK, BLOCK), 0) + kj * BLOCK
            i = lax.broadcasted_iota(jnp.int32, (BLOCK, BLOCK), 1) + qi * BLOCK
            allowed = allowed & (j <= i)
        for h in range(heads):
            c = head_cols(h)
            q, k, ga = q_ref[rq, c], kv_ref[rk, c], ga_ref[rq, c]
            half = nt(k, q) * half_scale + 0.5 * bias_ref[h]
            up = jnp.tanh(half) + 1.0
            act = half * up
            weights = jnp.where(allowed, act, 0.0).astype(jnp.bfloat16)
            acc[1, rk, c] += nn(weights, ga)
            slope = (act * (2.0 - up) + up) * half_scale
            grad_scores = jnp.where(allowed, nt(kv_ref[rv, c], ga) * slope, 0.0).astype(jnp.bfloat16)
            acc[0, rk, c] += nn(grad_scores, q)
            dq_ref[rq, c] += tn(grad_scores, k)

    each_pair(own, rows // BLOCK, rows // BLOCK, lo_ref, body)
    if first:
        term_ref[...] = acc[...].astype(jnp.bfloat16)


def middle_kernel(heads, att_ref, gates_ref, go_ref, w_ref, gg_ref, ga_ref, gw_ref):
    @pl.when(pl.program_id(0) == 0)
    def _():
        gw_ref[...] = jnp.zeros_like(gw_ref)

    go = go_ref[...]
    for h in range(heads):
        c = head_cols(h)
        grad_mixed = nt(go, w_ref[c, :])
        att = att_ref[:, c]
        gate = gates_ref[:, c].astype(jnp.float32)
        centered = att - jnp.mean(att, axis=-1, keepdims=True)
        inv_std = lax.rsqrt(jnp.mean(centered * centered, axis=-1, keepdims=True) + norm_eps)
        normed = centered * inv_std
        gw_ref[c, :] += tn((normed * gate).astype(jnp.bfloat16), go)
        gg_ref[:, c] = grad_mixed * normed
        grad_normed = grad_mixed * gate
        ga_ref[:, c] = (
            (
                grad_normed
                - jnp.mean(grad_normed, axis=-1, keepdims=True)
                - normed * jnp.mean(grad_normed * normed, axis=-1, keepdims=True)
            )
            * inv_std
        ).astype(jnp.bfloat16)


vmem = pl.BlockSpec(memory_space=pltpu.VMEM)
smem = pl.BlockSpec(memory_space=pltpu.SMEM)
kernel_params = pltpu.CompilerParams(vmem_limit_bytes=50 * 1024 * 1024)


def window_cost(own, rows, features, products):
    pairs = rows * rows // (2 if own else 1)
    return pl.CostEstimate(
        flops=4 * products * pairs * features,
        bytes_accessed=10 * rows * features,
        transcendentals=pairs * features // DH,
    )


def forward_window(own, lo, bias, q, kv, sq_col, sk_row, attended):
    rows, features = q.shape
    extra = () if own else (attended,)
    return pl.pallas_call(
        functools.partial(forward_kernel, own, features // DH),
        out_shape=jax.ShapeDtypeStruct((rows, features), jnp.float32),
        in_specs=[smem, smem] + [vmem] * (4 + len(extra)),
        out_specs=vmem,
        input_output_aliases={} if own else {6: 0},
        compiler_params=kernel_params,
        cost_estimate=window_cost(own, rows, features, 2),
    )(lo, bias, q, kv, sq_col, sk_row, *extra)


def backward_window(own, lo, bias, q, kv, ga, sq_row, sk_col, dq):
    rows, features = q.shape
    first = dq is None
    extra = () if first else (dq,)
    return pl.pallas_call(
        functools.partial(backward_kernel, own, features // DH),
        out_shape=(
            jax.ShapeDtypeStruct((rows, features), jnp.float32),
            jax.ShapeDtypeStruct((2, rows, features), jnp.bfloat16 if first else jnp.float32),
        ),
        in_specs=[smem, smem] + [vmem] * (5 + len(extra)),
        out_specs=(vmem, vmem),
        scratch_shapes=[pltpu.VMEM((2, rows, features), jnp.float32)] if first else [],
        input_output_aliases={} if first else {7: 0},
        compiler_params=kernel_params,
        cost_estimate=window_cost(own, rows, features, 5),
    )(lo, bias, q, kv, ga, sq_row, sk_col, *extra)


def middle(attended, gates, column_block, w_out):
    rows, features = attended.shape
    width = column_block.shape[1]
    by_rows = pl.BlockSpec((BLOCK, features), lambda i: (i, 0))
    whole = pl.BlockSpec((features, width), lambda i: (0, 0))
    return pl.pallas_call(
        functools.partial(middle_kernel, features // DH),
        grid=(rows // BLOCK,),
        out_shape=(
            jax.ShapeDtypeStruct((rows, features), jnp.float32),
            jax.ShapeDtypeStruct((rows, features), jnp.bfloat16),
            jax.ShapeDtypeStruct((features, width), jnp.float32),
        ),
        in_specs=[by_rows, by_rows, pl.BlockSpec((BLOCK, width), lambda i: (i, 0)), whole],
        out_specs=(by_rows, by_rows, whole),
        compiler_params=kernel_params,
        cost_estimate=pl.CostEstimate(
            flops=4 * rows * features * width, bytes_accessed=20 * rows * features, transcendentals=0
        ),
    )(attended, gates, column_block, w_out)


def per_device(queries, keys, values, gates, sessions, score_bias, grad_out, w_out):
    rows, features = queries.shape
    blocks = rows // BLOCK
    session_rows = -(-rows // features)
    my_index = lax.axis_index("seq")
    tail = jnp.zeros((16 * -(-session_rows // 16) * features,), jnp.bfloat16)
    tail = lax.dynamic_update_slice(tail, sessions.astype(jnp.bfloat16), (0,)).reshape(-1, features)
    packed = jnp.concatenate([keys, values, tail])
    first_of = sessions.reshape(blocks, BLOCK)[:, 0]
    sq_col = sessions.reshape(rows, 1)
    sq_row = sessions.reshape(blocks, 1, BLOCK)
    column_block = lax.all_gather(grad_out, "head", axis=1, tiled=True)

    windows, lows, attended, s = [], [], None, sessions
    for distance in (0,) + back_steps:
        windows.append((packed, s))
        last_of = s.reshape(blocks, BLOCK)[:, -1]
        lows.append(jnp.sum((last_of[None, :] < first_of[:, None]).astype(jnp.int32), axis=1))
        coming = shifted(packed, "seq", 1) if distance < 3 else None
        attended = forward_window(
            distance == 0, lows[distance], score_bias, queries, packed, sq_col,
            s.reshape(blocks, 1, BLOCK), attended,
        )
        if distance < 3:
            packed, attended = lax.optimization_barrier((coming, attended))
            s = packed[2 * rows :].reshape(-1)[:rows].astype(jnp.int32)
            s = jnp.where(my_index >= distance + 1, s, -1)
    grad_gates, grad_attended, product = middle(attended, gates, column_block, w_out)
    grad_w_out = lax.psum_scatter(product, "seq", scatter_dimension=1, tiled=True)

    grad_queries, sent = None, None
    for distance in (3, 2, 1, 0):
        kv, s = windows[distance]
        grad_queries, term = backward_window(
            distance == 0, lows[distance], score_bias, queries, kv, grad_attended, sq_row,
            s.reshape(rows, 1), grad_queries,
        )
        if sent is not None:
            term = term + sent.astype(jnp.float32)
        if distance:
            sent = shifted(term.astype(jnp.bfloat16), "seq", -1)
    return grad_queries, term[0], term[1], grad_gates, grad_w_out


def solution(mesh):
    return jax.shard_map(
        per_device,
        mesh=mesh,
        in_specs=(
            P("seq", "head"),
            P("seq", "head"),
            P("seq", "head"),
            P("seq", "head"),
            P("seq"),
            P("head"),
            P("seq", "head"),
            P("head", None),
        ),
        out_specs=(
            P("seq", "head"),
            P("seq", "head"),
            P("seq", "head"),
            P("seq", "head"),
            P("head", "seq"),
        ),
        check_vma=False,
    )
```

```python
import functools
import math

import jax
import jax.numpy as jnp
from jax import lax
from jax.experimental import pallas as pl
from jax.experimental.pallas import tpu as pltpu
from jax.sharding import PartitionSpec as P

DH = 128
BLOCK = 512

back_steps = (1, 2, 3)
norm_eps = 1e-05
half_scale = 0.5 / math.sqrt(DH)


def shifted(block, axis, distance):
    devices = range(lax.axis_size(axis))
    route = [(i - distance, i) for i in devices if i - distance in devices]
    return lax.ppermute(block, axis, route)


def nt(a, b):
    return lax.dot_general(a, b, (((1,), (1,)), ((), ())), preferred_element_type=jnp.float32)


def nn(a, b):
    return lax.dot_general(a, b, (((1,), (0,)), ((), ())), preferred_element_type=jnp.float32)


def tn(a, b):
    return lax.dot_general(a, b, (((0,), (0,)), ((), ())), preferred_element_type=jnp.float32)


def rows_of(index):
    return pl.ds(pl.multiple_of(index * BLOCK, BLOCK), BLOCK)


def head_cols(h):
    return slice(h * DH, (h + 1) * DH)


def each_pair(own, n_q, n_k, lo_ref, body):
    def over_q(qi, carry):
        def over_k(kj, inner):
            body(qi, kj)
            return inner

        lax.fori_loop(lo_ref[qi], qi + 1 if own else n_k, over_k, 0)
        return carry

    lax.fori_loop(0, n_q, over_q, 0)


def forward_kernel(own, heads, lo_ref, bias_ref, q_ref, k_ref, v_ref, sq_ref, sk_ref, *rest):
    rows = q_ref.shape[0]
    out_ref = rest[-1]
    if own:
        out_ref[...] = jnp.zeros_like(out_ref)
    else:
        out_ref[...] = rest[0][...]

    def body(qi, kj):
        rq, rk = rows_of(qi), rows_of(kj)
        allowed = sq_ref[rq, :] == sk_ref[kj]
        if own:
            i = lax.broadcasted_iota(jnp.int32, (BLOCK, BLOCK), 0) + qi * BLOCK
            j = lax.broadcasted_iota(jnp.int32, (BLOCK, BLOCK), 1) + kj * BLOCK
            allowed = allowed & (j <= i)
        raws = [nt(q_ref[rq, head_cols(h)], k_ref[rk, head_cols(h)]) for h in range(heads)]
        for h in range(heads):
            c = head_cols(h)
            half = raws[h] * half_scale + 0.5 * bias_ref[h]
            act = half * jnp.tanh(half) + half
            weights = jnp.where(allowed, act, 0.0).astype(jnp.bfloat16)
            out_ref[rq, c] += nn(weights, v_ref[rk, c])

    each_pair(own, rows // BLOCK, rows // BLOCK, lo_ref, body)


def backward_kernel(own, heads, lo_ref, bias_ref, q_ref, k_ref, v_ref, ga_ref, sq_ref, sk_ref, *rest):
    rows = q_ref.shape[0]
    first = rest[1].dtype == jnp.bfloat16
    if first:
        dq_ref, dk_ref, dv_ref, dk_acc, dv_acc = rest
        dq_ref[...] = jnp.zeros_like(dq_ref)
    else:
        dq_in, dq_ref, dk_acc, dv_acc = rest
        dq_ref[...] = dq_in[...]
    dk_acc[...] = jnp.zeros_like(dk_acc)
    dv_acc[...] = jnp.zeros_like(dv_acc)

    def body(qi, kj):
        rq, rk = rows_of(qi), rows_of(kj)
        allowed = sk_ref[rk, :] == sq_ref[qi]
        if own:
            j = lax.broadcasted_iota(jnp.int32, (BLOCK, BLOCK), 0) + kj * BLOCK
            i = lax.broadcasted_iota(jnp.int32, (BLOCK, BLOCK), 1) + qi * BLOCK
            allowed = allowed & (j <= i)
        for h in range(heads):
            c = head_cols(h)
            q, k, ga = q_ref[rq, c], k_ref[rk, c], ga_ref[rq, c]
            half = nt(k, q) * half_scale + 0.5 * bias_ref[h]
            up = jnp.tanh(half) + 1.0
            act = half * up
            weights = jnp.where(allowed, act, 0.0).astype(jnp.bfloat16)
            dv_acc[rk, c] += nn(weights, ga)
            slope = (act * (2.0 - up) + up) * half_scale
            grad_scores = jnp.where(allowed, nt(v_ref[rk, c], ga) * slope, 0.0).astype(jnp.bfloat16)
            dk_acc[rk, c] += nn(grad_scores, q)
            dq_ref[rq, c] += tn(grad_scores, k)

    each_pair(own, rows // BLOCK, rows // BLOCK, lo_ref, body)
    if first:
        dk_ref[...] = dk_acc[...].astype(jnp.bfloat16)
        dv_ref[...] = dv_acc[...].astype(jnp.bfloat16)


def middle_kernel(heads, att_ref, gates_ref, go_ref, w_ref, gg_ref, ga_ref, gw_ref):
    @pl.when(pl.program_id(0) == 0)
    def _():
        gw_ref[...] = jnp.zeros_like(gw_ref)

    go = go_ref[...]
    for h in range(heads):
        c = head_cols(h)
        grad_mixed = nt(go, w_ref[c, :])
        att = att_ref[:, c]
        gate = gates_ref[:, c].astype(jnp.float32)
        centered = att - jnp.mean(att, axis=-1, keepdims=True)
        inv_std = lax.rsqrt(jnp.mean(centered * centered, axis=-1, keepdims=True) + norm_eps)
        normed = centered * inv_std
        gw_ref[c, :] += tn((normed * gate).astype(jnp.bfloat16), go)
        gg_ref[:, c] = grad_mixed * normed
        grad_normed = grad_mixed * gate
        ga_ref[:, c] = (
            (
                grad_normed
                - jnp.mean(grad_normed, axis=-1, keepdims=True)
                - normed * jnp.mean(grad_normed * normed, axis=-1, keepdims=True)
            )
            * inv_std
        ).astype(jnp.bfloat16)


vmem = pl.BlockSpec(memory_space=pltpu.VMEM)
smem = pl.BlockSpec(memory_space=pltpu.SMEM)
kernel_params = pltpu.CompilerParams(vmem_limit_bytes=50 * 1024 * 1024)


def window_cost(own, rows, features, products):
    pairs = rows * rows // (2 if own else 1)
    return pl.CostEstimate(
        flops=4 * products * pairs * features,
        bytes_accessed=10 * rows * features,
        transcendentals=pairs * features // DH,
    )


def forward_window(own, lo, bias, q, k, v, sq_col, sk_row, attended):
    rows, features = q.shape
    extra = () if own else (attended,)
    return pl.pallas_call(
        functools.partial(forward_kernel, own, features // DH),
        out_shape=jax.ShapeDtypeStruct((rows, features), jnp.float32),
        in_specs=[smem, smem] + [vmem] * (5 + len(extra)),
        out_specs=vmem,
        input_output_aliases={} if own else {7: 0},
        compiler_params=kernel_params,
        cost_estimate=window_cost(own, rows, features, 2),
    )(lo, bias, q, k, v, sq_col, sk_row, *extra)


def backward_window(own, lo, bias, q, k, v, ga, sq_row, sk_col, dq):
    rows, features = q.shape
    first = dq is None
    extra = () if first else (dq,)
    term = jax.ShapeDtypeStruct((rows, features), jnp.bfloat16 if first else jnp.float32)
    return pl.pallas_call(
        functools.partial(backward_kernel, own, features // DH),
        out_shape=(
            jax.ShapeDtypeStruct((rows, features), jnp.float32),
            term,
            term,
        ),
        in_specs=[smem, smem] + [vmem] * (6 + len(extra)),
        out_specs=(vmem, vmem, vmem),
        scratch_shapes=[pltpu.VMEM((rows, features), jnp.float32)] * 2 if first else [],
        input_output_aliases={} if first else {8: 0},
        compiler_params=kernel_params,
        cost_estimate=window_cost(own, rows, features, 5),
    )(lo, bias, q, k, v, ga, sq_row, sk_col, *extra)


def middle(attended, gates, column_block, w_out):
    rows, features = attended.shape
    width = column_block.shape[1]
    by_rows = pl.BlockSpec((BLOCK, features), lambda i: (i, 0))
    whole = pl.BlockSpec((features, width), lambda i: (0, 0))
    return pl.pallas_call(
        functools.partial(middle_kernel, features // DH),
        grid=(rows // BLOCK,),
        out_shape=(
            jax.ShapeDtypeStruct((rows, features), jnp.float32),
            jax.ShapeDtypeStruct((rows, features), jnp.bfloat16),
            jax.ShapeDtypeStruct((features, width), jnp.float32),
        ),
        in_specs=[by_rows, by_rows, pl.BlockSpec((BLOCK, width), lambda i: (i, 0)), whole],
        out_specs=(by_rows, by_rows, whole),
        compiler_params=kernel_params,
        cost_estimate=pl.CostEstimate(
            flops=4 * rows * features * width, bytes_accessed=20 * rows * features, transcendentals=0
        ),
    )(attended, gates, column_block, w_out)


def per_device(queries, keys, values, gates, sessions, score_bias, grad_out, w_out):
    rows, features = queries.shape
    blocks = rows // BLOCK
    session_rows = -(-rows // features)
    my_index = lax.axis_index("seq")
    tail = jnp.zeros((16 * -(-session_rows // 16) * features,), jnp.bfloat16)
    tail = lax.dynamic_update_slice(tail, sessions.astype(jnp.bfloat16), (0,)).reshape(-1, features)
    k, v = keys, jnp.concatenate([values, tail])
    first_of = sessions.reshape(blocks, BLOCK)[:, 0]
    sq_col = sessions.reshape(rows, 1)
    sq_row = sessions.reshape(blocks, 1, BLOCK)
    column_block = lax.all_gather(grad_out, "head", axis=1, tiled=True)

    windows, lows, attended, s = [], [], None, sessions
    for distance in (0,) + back_steps:
        windows.append((k, v, s))
        last_of = s.reshape(blocks, BLOCK)[:, -1]
        lows.append(jnp.sum((last_of[None, :] < first_of[:, None]).astype(jnp.int32), axis=1))
        if distance < 3:
            k_coming, v_coming = shifted(k, "seq", 1), shifted(v, "seq", 1)
        attended = forward_window(
            distance == 0, lows[distance], score_bias, queries, k, v, sq_col,
            s.reshape(blocks, 1, BLOCK), attended,
        )
        if distance < 3:
            k, attended = lax.optimization_barrier((k_coming, attended))
            v, attended = lax.optimization_barrier((v_coming, attended))
            s = v[rows:].reshape(-1)[:rows].astype(jnp.int32)
            s = jnp.where(my_index >= distance + 1, s, -1)
    grad_gates, grad_attended, product = middle(attended, gates, column_block, w_out)
    grad_w_out = lax.psum_scatter(product, "seq", scatter_dimension=1, tiled=True)

    grad_queries, sent = None, None
    for distance in (3, 2, 1, 0):
        k, v, s = windows[distance]
        grad_queries, *terms = backward_window(
            distance == 0, lows[distance], score_bias, queries, k, v, grad_attended, sq_row,
            s.reshape(rows, 1), grad_queries,
        )
        if sent is not None:
            terms = [term + part.astype(jnp.float32) for term, part in zip(terms, sent)]
        if distance:
            sent = [shifted(term.astype(jnp.bfloat16), "seq", -1) for term in terms]
    return grad_queries, terms[0], terms[1], grad_gates, grad_w_out


def solution(mesh):
    return jax.shard_map(
        per_device,
        mesh=mesh,
        in_specs=(
            P("seq", "head"),
            P("seq", "head"),
            P("seq", "head"),
            P("seq", "head"),
            P("seq"),
            P("head"),
            P("seq", "head"),
            P("head", None),
        ),
        out_specs=(
            P("seq", "head"),
            P("seq", "head"),
            P("seq", "head"),
            P("seq", "head"),
            P("head", "seq"),
        ),
        check_vma=False,
    )
```

```python
import functools
import math

import jax
import jax.numpy as jnp
from jax import lax
from jax.experimental import pallas as pl
from jax.experimental.pallas import tpu as pltpu
from jax.sharding import PartitionSpec as P

DH = 128
BLOCK = 512

back_steps = (1, 2, 3)
norm_eps = 1e-05
half_scale = 0.5 / math.sqrt(DH)


def shifted(block, axis, distance):
    devices = range(lax.axis_size(axis))
    route = [(i - distance, i) for i in devices if i - distance in devices]
    return lax.ppermute(block, axis, route)


def nt(a, b):
    return lax.dot_general(a, b, (((1,), (1,)), ((), ())), preferred_element_type=jnp.float32)


def nn(a, b):
    return lax.dot_general(a, b, (((1,), (0,)), ((), ())), preferred_element_type=jnp.float32)


def tn(a, b):
    return lax.dot_general(a, b, (((0,), (0,)), ((), ())), preferred_element_type=jnp.float32)


def rows_of(index):
    return pl.ds(pl.multiple_of(index * BLOCK, BLOCK), BLOCK)


def head_cols(h):
    return slice(h * DH, (h + 1) * DH)


def each_pair(own, n_q, n_k, lo_ref, body):
    def over_q(qi, carry):
        def over_k(kj, inner):
            body(qi, kj)
            return inner

        lax.fori_loop(lo_ref[qi], qi + 1 if own else n_k, over_k, 0)
        return carry

    lax.fori_loop(0, n_q, over_q, 0)


def forward_kernel(own, heads, lo_ref, bias_ref, q_ref, k_ref, v_ref, sq_ref, sk_ref, *rest):
    rows = q_ref.shape[0]
    out_ref = rest[-1]
    if own:
        out_ref[...] = jnp.zeros_like(out_ref)
    else:
        out_ref[...] = rest[0][...]

    def body(qi, kj):
        rq, rk = rows_of(qi), rows_of(kj)
        allowed = sq_ref[rq, :] == sk_ref[kj]
        if own:
            i = lax.broadcasted_iota(jnp.int32, (BLOCK, BLOCK), 0) + qi * BLOCK
            j = lax.broadcasted_iota(jnp.int32, (BLOCK, BLOCK), 1) + kj * BLOCK
            allowed = allowed & (j <= i)
        raws = [nt(q_ref[rq, head_cols(h)], k_ref[rk, head_cols(h)]) for h in range(heads)]
        for h in range(heads):
            c = head_cols(h)
            half = raws[h] * half_scale + 0.5 * bias_ref[h]
            act = half * jnp.tanh(half) + half
            weights = jnp.where(allowed, act, 0.0).astype(jnp.bfloat16)
            out_ref[rq, c] += nn(weights, v_ref[rk, c])

    each_pair(own, rows // BLOCK, rows // BLOCK, lo_ref, body)


def backward_kernel(own, heads, lo_ref, bias_ref, q_ref, k_ref, v_ref, ga_ref, sq_ref, sk_ref, *rest):
    rows = q_ref.shape[0]
    first = rest[1].dtype == jnp.bfloat16
    if first:
        dq_ref, dk_ref, dv_ref, dk_acc, dv_acc = rest
        dq_ref[...] = jnp.zeros_like(dq_ref)
    else:
        dq_in, dq_ref, dk_acc, dv_acc = rest
        dq_ref[...] = dq_in[...]
    dk_acc[...] = jnp.zeros_like(dk_acc)
    dv_acc[...] = jnp.zeros_like(dv_acc)

    def body(qi, kj):
        rq, rk = rows_of(qi), rows_of(kj)
        allowed = sk_ref[rk, :] == sq_ref[qi]
        if own:
            j = lax.broadcasted_iota(jnp.int32, (BLOCK, BLOCK), 0) + kj * BLOCK
            i = lax.broadcasted_iota(jnp.int32, (BLOCK, BLOCK), 1) + qi * BLOCK
            allowed = allowed & (j <= i)
        def products(h):
            c = head_cols(h)
            return nt(k_ref[rk, c], q_ref[rq, c]), nt(v_ref[rk, c], ga_ref[rq, c])

        ahead = products(0)
        for h in range(heads):
            c = head_cols(h)
            raw, grad_weights = ahead
            if h + 1 < heads:
                ahead = products(h + 1)
            half = raw * half_scale + 0.5 * bias_ref[h]
            up = jnp.tanh(half) + 1.0
            act = half * up
            weights = jnp.where(allowed, act, 0.0).astype(jnp.bfloat16)
            slope = (act * (2.0 - up) + up) * half_scale
            grad_scores = jnp.where(allowed, grad_weights * slope, 0.0).astype(jnp.bfloat16)
            dv_acc[rk, c] += nn(weights, ga_ref[rq, c])
            dk_acc[rk, c] += nn(grad_scores, q_ref[rq, c])
            dq_ref[rq, c] += tn(grad_scores, k_ref[rk, c])

    each_pair(own, rows // BLOCK, rows // BLOCK, lo_ref, body)
    if first:
        dk_ref[...] = dk_acc[...].astype(jnp.bfloat16)
        dv_ref[...] = dv_acc[...].astype(jnp.bfloat16)


def middle_kernel(heads, att_ref, gates_ref, go_ref, w_ref, gg_ref, ga_ref, gw_ref):
    @pl.when(pl.program_id(0) == 0)
    def _():
        gw_ref[...] = jnp.zeros_like(gw_ref)

    go = go_ref[...]
    for h in range(heads):
        c = head_cols(h)
        grad_mixed = nt(go, w_ref[c, :])
        att = att_ref[:, c]
        gate = gates_ref[:, c].astype(jnp.float32)
        centered = att - jnp.mean(att, axis=-1, keepdims=True)
        inv_std = lax.rsqrt(jnp.mean(centered * centered, axis=-1, keepdims=True) + norm_eps)
        normed = centered * inv_std
        gw_ref[c, :] += tn((normed * gate).astype(jnp.bfloat16), go)
        gg_ref[:, c] = grad_mixed * normed
        grad_normed = grad_mixed * gate
        ga_ref[:, c] = (
            (
                grad_normed
                - jnp.mean(grad_normed, axis=-1, keepdims=True)
                - normed * jnp.mean(grad_normed * normed, axis=-1, keepdims=True)
            )
            * inv_std
        ).astype(jnp.bfloat16)


vmem = pl.BlockSpec(memory_space=pltpu.VMEM)
smem = pl.BlockSpec(memory_space=pltpu.SMEM)
kernel_params = pltpu.CompilerParams(vmem_limit_bytes=50 * 1024 * 1024)


def window_cost(own, rows, features, products):
    pairs = rows * rows // (2 if own else 1)
    return pl.CostEstimate(
        flops=4 * products * pairs * features,
        bytes_accessed=10 * rows * features,
        transcendentals=pairs * features // DH,
    )


def forward_window(own, lo, bias, q, k, v, sq_col, sk_row, attended):
    rows, features = q.shape
    extra = () if own else (attended,)
    return pl.pallas_call(
        functools.partial(forward_kernel, own, features // DH),
        out_shape=jax.ShapeDtypeStruct((rows, features), jnp.float32),
        in_specs=[smem, smem] + [vmem] * (5 + len(extra)),
        out_specs=vmem,
        input_output_aliases={} if own else {7: 0},
        compiler_params=kernel_params,
        cost_estimate=window_cost(own, rows, features, 2),
    )(lo, bias, q, k, v, sq_col, sk_row, *extra)


def backward_window(own, lo, bias, q, k, v, ga, sq_row, sk_col, dq):
    rows, features = q.shape
    first = dq is None
    extra = () if first else (dq,)
    term = jax.ShapeDtypeStruct((rows, features), jnp.bfloat16 if first else jnp.float32)
    return pl.pallas_call(
        functools.partial(backward_kernel, own, features // DH),
        out_shape=(
            jax.ShapeDtypeStruct((rows, features), jnp.float32),
            term,
            term,
        ),
        in_specs=[smem, smem] + [vmem] * (6 + len(extra)),
        out_specs=(vmem, vmem, vmem),
        scratch_shapes=[pltpu.VMEM((rows, features), jnp.float32)] * 2 if first else [],
        input_output_aliases={} if first else {8: 0},
        compiler_params=kernel_params,
        cost_estimate=window_cost(own, rows, features, 5),
    )(lo, bias, q, k, v, ga, sq_row, sk_col, *extra)


def middle(attended, gates, column_block, w_out):
    rows, features = attended.shape
    width = column_block.shape[1]
    by_rows = pl.BlockSpec((BLOCK, features), lambda i: (i, 0))
    whole = pl.BlockSpec((features, width), lambda i: (0, 0))
    return pl.pallas_call(
        functools.partial(middle_kernel, features // DH),
        grid=(rows // BLOCK,),
        out_shape=(
            jax.ShapeDtypeStruct((rows, features), jnp.float32),
            jax.ShapeDtypeStruct((rows, features), jnp.bfloat16),
            jax.ShapeDtypeStruct((features, width), jnp.float32),
        ),
        in_specs=[by_rows, by_rows, pl.BlockSpec((BLOCK, width), lambda i: (i, 0)), whole],
        out_specs=(by_rows, by_rows, whole),
        compiler_params=kernel_params,
        cost_estimate=pl.CostEstimate(
            flops=4 * rows * features * width, bytes_accessed=20 * rows * features, transcendentals=0
        ),
    )(attended, gates, column_block, w_out)


def per_device(queries, keys, values, gates, sessions, score_bias, grad_out, w_out):
    rows, features = queries.shape
    blocks = rows // BLOCK
    session_rows = -(-rows // features)
    my_index = lax.axis_index("seq")
    tail = jnp.zeros((16 * -(-session_rows // 16) * features,), jnp.bfloat16)
    tail = lax.dynamic_update_slice(tail, sessions.astype(jnp.bfloat16), (0,)).reshape(-1, features)
    k, v = keys, jnp.concatenate([values, tail])
    first_of = sessions.reshape(blocks, BLOCK)[:, 0]
    sq_col = sessions.reshape(rows, 1)
    sq_row = sessions.reshape(blocks, 1, BLOCK)
    column_block = lax.all_gather(grad_out, "head", axis=1, tiled=True)

    windows, lows, attended, s = [], [], None, sessions
    for distance in (0,) + back_steps:
        windows.append((k, v, s))
        last_of = s.reshape(blocks, BLOCK)[:, -1]
        lows.append(jnp.sum((last_of[None, :] < first_of[:, None]).astype(jnp.int32), axis=1))
        if distance < 3:
            k_coming, v_coming = shifted(k, "seq", 1), shifted(v, "seq", 1)
        attended = forward_window(
            distance == 0, lows[distance], score_bias, queries, k, v, sq_col,
            s.reshape(blocks, 1, BLOCK), attended,
        )
        if distance < 3:
            k, attended = lax.optimization_barrier((k_coming, attended))
            v, attended = lax.optimization_barrier((v_coming, attended))
            s = v[rows:].reshape(-1)[:rows].astype(jnp.int32)
            s = jnp.where(my_index >= distance + 1, s, -1)
    grad_gates, grad_attended, product = middle(attended, gates, column_block, w_out)
    grad_w_out = lax.psum_scatter(product, "seq", scatter_dimension=1, tiled=True)

    grad_queries, sent = None, None
    for distance in (3, 2, 1, 0):
        k, v, s = windows[distance]
        grad_queries, *terms = backward_window(
            distance == 0, lows[distance], score_bias, queries, k, v, grad_attended, sq_row,
            s.reshape(rows, 1), grad_queries,
        )
        if sent is not None:
            terms = [term + part.astype(jnp.float32) for term, part in zip(terms, sent)]
        if distance:
            sent = [shifted(term.astype(jnp.bfloat16), "seq", -1) for term in terms]
    return grad_queries, terms[0], terms[1], grad_gates, grad_w_out


def solution(mesh):
    return jax.shard_map(
        per_device,
        mesh=mesh,
        in_specs=(
            P("seq", "head"),
            P("seq", "head"),
            P("seq", "head"),
            P("seq", "head"),
            P("seq"),
            P("head"),
            P("seq", "head"),
            P("head", None),
        ),
        out_specs=(
            P("seq", "head"),
            P("seq", "head"),
            P("seq", "head"),
            P("seq", "head"),
            P("head", "seq"),
        ),
        check_vma=False,
    )
```
